32 devices in a mesh: gx: 8 (over z, x), gy: 2 (over core), gz: 2 (over y).
Axes of the slice: x: 2, y: 2, z: 4, core: 2. Of those that a mesh axis runs over, the one named last changes fastest.
Arguments:
- velocity: bfloat16 [3, 16, 16, 256], P(None, 'gx', 'gy', 'gz'), may hold values from -6 to 6
- eddy_viscosity: float32 [16, 16, 256], P('gx', 'gy', 'gz'), may hold values from 0.02 to 0.3
- cell_owner: int32 [2, 2, 16384, 1], P('gy', 'gz', 'gx'), may hold values from 0 to 7; in each aligned block of 2048 rows (0 to 2047, 2048 to 4095, ..., all dimensions but the last counted through in order) at most 384 rows name the same one
- cell_element: int32 [2, 2, 16384], P('gy', 'gz', 'gx'), may hold values from 0 to 3
- cell_position: int32 [2, 2, 16384], P('gy', 'gz', 'gx'), may hold values from 0 to 4095
- acoustic_state: float32 [4, 8, 2, 8, 512], P(None, 'gx', 'gy', 'gz'), may hold values from -6 to 6
Outputs:
- source_moments: float32 [8, 2, 8, 3, 512], P('gx', 'gy', 'gz')
- next_state: float32 [4, 8, 2, 8, 512], P(None, 'gx', 'gy', 'gz')
The draws below stay inside these ranges and needn't reach their ends.
Inputs may be any that keep to these rules, and one draw needn't show every extreme that they name: `cell_owner`: in the rows of one device (aligned blocks of 2048 rows along the last two dimensions), no owner is named more than 384 times, a bound that some block reaches.
All inputs are finite; a program needn't handle non-finite values.
Results may differ from the reference program's by a relative error of at most 0.0039.
Values may be sent and summed in bfloat16 or wider, within the bound.
A program may use at most 64 MiB of HBM per device.

```python
import math
import jax
import jax.numpy as jnp
import numpy as np
from jax import lax

CX = 2
CY = 8
CZ = 128
EX = 1
EY = 1
EZ = 4
SUB = 16
NODES = 512
CELLS = 2048
CAP = 384
ELEMS_DEV = 4
NX = 16
NY = 16
NZ = 256
EGX = 8
EGY = 2
EGZ = 8
N_GX = 8
N_GY = 2
N_GZ = 2


def plant(values, rng, least, top_value):
    place = [jax.random.randint(jax.random.fold_in(rng, axis), (), 0, length) for axis, length in enumerate(values.shape)]
    widest = values.shape.index(max(values.shape))
    beside = place[:widest] + [(place[widest] + 1) % values.shape[widest]] + place[widest + 1:]
    return values.at[tuple(place)].set(least).at[tuple(beside)].set(top_value)


def block_scale(key, shape, shards, smallest, high):
    def one(position, parts):
        steps = jax.random.uniform(jax.random.fold_in(jax.random.fold_in(key, 6), position), (parts,), jnp.float32, smallest / len(shards), high / len(shards))
        return jnp.repeat(jnp.exp(steps), shape[position] // parts).reshape((-1,) + (1,) * (len(shape) - position - 1))

    loudness = one(*shards[0])
    for cut in shards[1:]:
        loudness = loudness * one(*cut)
    return loudness


def shared_out(stream_key, own, number, rows, number_of, top, bound, slope):
    sequence = jax.random.permutation(stream_key, number_of)
    packed, common = shares(number_of, rows * top, bound, slope, True), shares(number_of, rows * top, bound, slope, False)
    places = jnp.arange(number_of)

    def named(sizes, offset_by):
        used = int((sizes > 0).sum())
        fixed = max(1, used // 4)
        moved = fixed + (places - fixed + offset_by * (used - fixed)) % max(1, number_of - fixed)
        return jnp.zeros((number_of,), jnp.int32).at[sequence[jnp.where(places < fixed, places, moved)]].set(jnp.asarray(sizes, jnp.int32))

    sizes = jnp.where(number % 4 == 0, named(packed, number // 4), named(common, number - number // 4 - 1))
    mixed = jax.random.permutation(jax.random.fold_in(own, 3), number_of)
    giver, taker = mixed[0:number_of // 2 * 2:2], mixed[1:number_of // 2 * 2:2]
    slack = jnp.minimum(sizes[giver] - 1, bound - sizes[taker]) // 2
    slack = jnp.where((giver == sequence[0]) | (taker == sequence[0]) | (sizes[taker] == 0), 0, jnp.maximum(slack, 0))
    moved = jax.random.randint(jax.random.fold_in(own, 4), (number_of // 2,), 0, 1 << 20) % (slack + 1)
    sizes = sizes.at[giver].add(-moved).at[taker].add(moved)
    members = jnp.searchsorted(jnp.cumsum(sizes), jnp.arange(rows * top), side="right").astype(jnp.int32)
    table = members.reshape(top, rows).T
    table = table[jax.random.permutation(jax.random.fold_in(own, 1), rows)]
    offset_by = jax.random.randint(jax.random.fold_in(own, 2), (rows, 1), 0, top)
    return jnp.take_along_axis(table, (jnp.arange(top)[None, :] + offset_by) % top, axis=1)


def shares(count, total, limit, slope, full):
    weights = [(1 << 20) // math.isqrt(standing ** slope) + 1 for standing in range(1, count + 1)]
    largest = limit if full else min(limit, max(-(-total // count), total * weights[0] // sum(weights)))
    least = 1 if total - largest >= count - 1 else 0
    given, surplus = [largest] + [least] * (count - 1), total - largest - least * (count - 1)
    while surplus > 0:
        movable = [i for i in range(1, count) if given[i] < largest] or [i for i in range(1, count) if given[i] < limit]
        pool, left = sum([weights[i] for i in movable]), surplus
        for i in movable:
            more = min(limit - given[i], max(1, left * weights[i] // pool), surplus)
            given[i] = given[i] + more
            surplus = surplus - more
    return np.array(given)


def centred(rng, dims, deviation, reach, split=(), kind=jnp.bfloat16):
    drawn = jax.random.normal(rng, dims, jnp.float32) * deviation
    if len(split) > 0:
        drawn = block_scale(rng, dims, split, -0.22, 0.18) * drawn
    return jnp.clip(drawn, min=-reach, max=reach).astype(kind)


def setup_inputs(seed: int = 0) -> dict:
    seeds = jax.random.split(jax.random.key(seed), 7)
    velocity = centred(seeds[0], (3, NX, NY, NZ), 1.0, 6.0, ((1, 8), (2, 2), (3, 2)))
    eddy_viscosity = jnp.clip(jnp.exp(math.log(0.3) - 2.7080503 * jax.random.uniform(seeds[1], (NX, NY, NZ), jnp.float32) ** block_scale(seeds[1], (NX, NY, NZ), ((0, 8), (1, 2), (2, 2)), -0.2, 0.2)), 0.02, 0.3)
    cell_owner_keys = jax.random.split(jax.random.fold_in(seeds[2], 1), N_GY * N_GZ * (N_GX * CELLS) // CELLS)
    cell_owner_turns = jax.random.permutation(jax.random.fold_in(seeds[2], 3), N_GY * N_GZ * (N_GX * CELLS) // CELLS)
    cell_owner = jax.vmap(lambda own, number: shared_out(jax.random.fold_in(seeds[2], 2), own, number, CELLS, N_GX, 1, CAP, 1))(cell_owner_keys, cell_owner_turns).reshape((N_GY, N_GZ, N_GX * CELLS, 1))
    cell_element = plant(jax.random.randint(seeds[3], (N_GY, N_GZ, N_GX * CELLS), 0, ELEMS_DEV), jax.random.fold_in(seeds[3], 1), 0, ELEMS_DEV - 1).astype(jnp.int32)
    cell_position = plant(jax.random.randint(seeds[4], (N_GY, N_GZ, N_GX * CELLS), 0, SUB * SUB * SUB), jax.random.fold_in(seeds[4], 1), 0, (SUB * SUB * SUB) - 1).astype(jnp.int32)
    acoustic_state = centred(seeds[5], (4, EGX, EGY, EGZ, NODES), 1.0, 6.0, ((1, 8), (2, 2), (3, 2)), jnp.float32)
    return {"velocity": velocity, "eddy_viscosity": eddy_viscosity, "cell_owner": cell_owner, "cell_element": cell_element, "cell_position": cell_position, "acoustic_state": acoustic_state}


GLL_POINTS = np.array([-1.0, -0.8717401485096066, -0.5917001814331423, -0.2092992179024789, 0.2092992179024789, 0.5917001814331423, 0.8717401485096066, 1.0])
LIFT_FACTOR = 28.0
TIME_STEP = 0.01
COUPLING = 4.0
MOMENT_WEIGHT = 0.0625


def derivative_matrix():
    points = GLL_POINTS
    barycentric = np.ones(8)
    for j in range(8):
        for m in range(8):
            if m != j:
                barycentric[j] = barycentric[j] / (points[j] - points[m])
    matrix = np.zeros((8, 8))
    for i in range(8):
        for j in range(8):
            if i != j:
                matrix[i, j] = barycentric[j] / barycentric[i] / (points[i] - points[j])
        matrix[i, i] = -np.sum(matrix[i])
    return matrix


def kron_tables():
    matrix = derivative_matrix()
    identity = np.eye(8)
    along_x = np.kron(np.kron(matrix, identity), identity).T
    along_y = np.kron(np.kron(identity, matrix), identity).T
    along_z = np.kron(np.kron(identity, identity), matrix).T
    return [jnp.asarray(t, dtype=jnp.float32) for t in (along_x, along_y, along_z)]


def basis_table():
    points = GLL_POINTS
    centres = -1.0 + (2.0 * np.arange(SUB) + 1.0) / SUB
    values = np.ones((SUB, 8))
    for j in range(8):
        for m in range(8):
            if m != j:
                values[:, j] = values[:, j] * (centres - points[m]) / (points[j] - points[m])
    return jnp.asarray(values, dtype=jnp.float32)


def source_from_padded(padded, viscosity):
    centre = padded[:, 1:-1, 1:-1, 1:-1]
    plus_x = padded[:, 2:, 1:-1, 1:-1]
    minus_x = padded[:, :-2, 1:-1, 1:-1]
    plus_y = padded[:, 1:-1, 2:, 1:-1]
    minus_y = padded[:, 1:-1, :-2, 1:-1]
    plus_z = padded[:, 1:-1, 1:-1, 2:]
    minus_z = padded[:, 1:-1, 1:-1, :-2]
    grad_x = 0.5 * (plus_x - minus_x)
    grad_y = 0.5 * (plus_y - minus_y)
    grad_z = 0.5 * (plus_z - minus_z)
    laplace = plus_x + minus_x + plus_y + minus_y + plus_z + minus_z - 6.0 * centre
    curl_x = grad_y[2] - grad_z[1]
    curl_y = grad_z[0] - grad_x[2]
    curl_z = grad_x[1] - grad_y[0]
    lamb_x = curl_y * centre[2] - curl_z * centre[1]
    lamb_y = curl_z * centre[0] - curl_x * centre[2]
    lamb_z = curl_x * centre[1] - curl_y * centre[0]
    lamb = jnp.stack([lamb_x, lamb_y, lamb_z])
    return (viscosity[None] * laplace - lamb).astype(jnp.bfloat16)


def face_correction(inside, outside, normal, component):
    difference = inside - outside
    result = -0.5 * difference
    result = result.at[0].add(0.5 * normal * difference[component])
    result = result.at[component].add(0.5 * normal * difference[0])
    return LIFT_FACTOR * result


def tendency(fields, forcing, tables, exterior):
    highest = lax.Precision.HIGHEST
    pressure = fields[0]
    grad_x = jnp.dot(pressure, tables[0], precision=highest)
    grad_y = jnp.dot(pressure, tables[1], precision=highest)
    grad_z = jnp.dot(pressure, tables[2], precision=highest)
    divergence = jnp.dot(fields[1], tables[0], precision=highest) + jnp.dot(fields[2], tables[1], precision=highest) + jnp.dot(fields[3], tables[2], precision=highest)
    result = jnp.stack([-divergence, COUPLING * forcing[0] - grad_x, COUPLING * forcing[1] - grad_y, COUPLING * forcing[2] - grad_z])
    shape_now = fields.shape
    nodal_view = fields.reshape(shape_now[:4] + (8, 8, 8))
    result = result.reshape(nodal_view.shape)
    for direction in range(3):
        node_axis = 4 + direction
        lower_face = jnp.take(nodal_view, 0, axis=node_axis)
        upper_face = jnp.take(nodal_view, 7, axis=node_axis)
        lower_outer, upper_outer = exterior(lower_face, upper_face, direction)
        leading = (slice(None),) * node_axis
        result = result.at[leading + (0,)].add(face_correction(lower_face, lower_outer, -1.0, direction + 1))
        result = result.at[leading + (7,)].add(face_correction(upper_face, upper_outer, 1.0, direction + 1))
    return result.reshape(shape_now)


def runge_kutta(fields, forcing, exterior):
    tables = kron_tables()
    section_one = fields + TIME_STEP * tendency(fields, forcing, tables, exterior)
    section_two = 0.75 * fields + 0.25 * (section_one + TIME_STEP * tendency(section_one, forcing, tables, exterior))
    return (1.0 / 3.0) * fields + (2.0 / 3.0) * (section_two + TIME_STEP * tendency(section_two, forcing, tables, exterior))


def zero_exterior(lower_face, upper_face, direction):
    elem_axis = direction + 1
    extent = lower_face.shape[elem_axis]
    zero_rim = jnp.zeros_like(lax.slice_in_dim(lower_face, 0, 1, axis=elem_axis))
    lower_outer = jnp.concatenate([zero_rim, lax.slice_in_dim(upper_face, 0, extent - 1, axis=elem_axis)], axis=elem_axis)
    upper_outer = jnp.concatenate([lax.slice_in_dim(lower_face, 1, extent, axis=elem_axis), zero_rim], axis=elem_axis)
    return lower_outer, upper_outer


def position_rows():
    values = basis_table()
    node_rows = (values[:, None, None, :, None, None] * values[None, :, None, None, :, None]) * values[None, None, :, None, None, :]
    return node_rows.reshape(SUB * SUB * SUB, NODES).astype(jnp.bfloat16)


def reference(velocity, eddy_viscosity, cell_owner, cell_element, cell_position, acoustic_state):
    padded = jnp.pad(velocity.astype(jnp.float32), ((0, 0), (1, 1), (1, 1), (1, 1)))
    sources = source_from_padded(padded, eddy_viscosity)
    columns = N_GY * N_GZ
    cell_count = CX * CY * CZ
    subcells = SUB * SUB * SUB
    ordered = sources.astype(jnp.float32).reshape(3, N_GX, CX, N_GY, CY, N_GZ, CZ)
    ordered = jnp.transpose(ordered, (3, 5, 1, 2, 4, 6, 0)).reshape(columns, N_GX * cell_count, 3)
    owners = cell_owner.reshape(columns, N_GX * cell_count)
    elements = cell_element.reshape(columns, N_GX * cell_count)
    positions = cell_position.reshape(columns, N_GX * cell_count)
    weight_rows = position_rows().astype(jnp.float32)

    def column_moments(column_items):
        column_source, column_owner, column_element, column_position = column_items
        segment_ids = (column_owner * ELEMS_DEV + column_element) * subcells + column_position
        totals = jax.ops.segment_sum(column_source, segment_ids, num_segments=N_GX * ELEMS_DEV * subcells)
        totals = totals.reshape(N_GX * ELEMS_DEV, subcells, 3)
        return jnp.einsum('gpc,pn->gcn', totals, weight_rows, precision=lax.Precision.HIGHEST)

    moments = lax.map(column_moments, (ordered, owners, elements, positions))
    moments = moments * MOMENT_WEIGHT
    moments = moments.reshape(N_GY, N_GZ, N_GX, EX, EY, EZ, 3, NODES)
    moments = jnp.transpose(moments, (2, 3, 0, 4, 1, 5, 6, 7)).reshape(EGX, EGY, EGZ, 3, NODES)
    forcing = jnp.moveaxis(moments, 3, 0)
    next_state = runge_kutta(acoustic_state, forcing, zero_exterior)
    return moments, next_state
```

```python
import functools

import jax
import jax.numpy as jnp
import numpy as np
from jax import lax
from jax.experimental import pallas as pl
from jax.experimental.pallas import tpu as pltpu
from jax.sharding import PartitionSpec as P

MESH = pl.DeviceIdType.MESH
SUB = 16
NODES = 512
LANES = 128
TILES = NODES // LANES
BLOCK = 8
GLL_POINTS = np.array(
    [
        -1.0,
        -0.8717401485096066,
        -0.5917001814331423,
        -0.2092992179024789,
        0.2092992179024789,
        0.5917001814331423,
        0.8717401485096066,
        1.0,
    ]
)
HALF_LIFT = 14.0
TIME_STEP = 0.01
COUPLING = 4.0
MOMENT_WEIGHT = 0.0625


def derivative_matrix():
    points = GLL_POINTS
    barycentric = np.ones(8)
    for j in range(8):
        for m in range(8):
            if m != j:
                barycentric[j] = barycentric[j] / (points[j] - points[m])
    matrix = np.zeros((8, 8))
    for i in range(8):
        for j in range(8):
            if i != j:
                matrix[i, j] = barycentric[j] / barycentric[i] / (points[i] - points[j])
        matrix[i, i] = -np.sum(matrix[i])
    return matrix


def basis_values():
    points = GLL_POINTS
    centres = -1.0 + (2.0 * np.arange(SUB) + 1.0) / SUB
    values = np.ones((SUB, 8))
    for j in range(8):
        for m in range(8):
            if m != j:
                values[:, j] = values[:, j] * (centres - points[m]) / (points[j] - points[m])
    return values


def constant_table():
    along = -derivative_matrix()
    along[0, 0] -= HALF_LIFT
    along[7, 7] += HALF_LIFT
    table = np.zeros((168, 2 * LANES))
    table[:128, :128] = np.kron(np.eye(2), np.kron(along, np.eye(8))).T
    table[:128, 128:] = np.kron(np.eye(16), along).T
    for j in range(TILES):
        for i in range(TILES):
            for h in range(2):
                lanes = slice(64 * h, 64 * h + 64)
                table[128 + 8 * j + 2 * i, lanes] = along[2 * j + h, 2 * i + h]
                table[129 + 8 * j + 2 * i, lanes] = along[2 * j + h, 2 * i + 1 - h]
    table[160:168, :SUB] = basis_values().T
    return table.astype(np.float32)


def each(count, body):
    if count <= 16:
        for k in range(count):
            body(k)
    else:
        lax.fori_loop(0, count, lambda k, c: (body(k), c)[1], 0)


def kernel(
    n,
    vel_ref, visc_ref, own_ref, elem_ref, pos_ref, state_ref, table_ref,
    mom_ref, next_ref,
    vel_in, state0, state1, state2, left_in, right_in, y_in, z_in,
    nodes, part, psend, precv,
    vel_send_sem, vel_recv_sem, face_send_sem, face_recv_sem, part_send_sem, part_recv_sem,
):
    f32 = jnp.float32
    gx, gy, gz = lax.axis_index("gx"), lax.axis_index("gy"), lax.axis_index("gz")
    last = n - 1
    has_left, has_right = gx > 0, gx < last
    low_y, low_z = gy == 0, gz == 0
    left = {"gx": jnp.maximum(gx - 1, 0)}
    right = {"gx": jnp.minimum(gx + 1, last)}
    other_y, other_z = {"gy": 1 - gy}, {"gz": 1 - gz}

    def peer(k):
        return lax.rem(gx + 1 + k, n)

    barrier = pltpu.get_barrier_semaphore()
    each(last, lambda k: pl.semaphore_signal(barrier, inc=1, device_id={"gx": peer(k)}, device_id_type=MESH))
    pl.semaphore_signal(barrier, inc=1, device_id=other_y, device_id_type=MESH)
    pl.semaphore_signal(barrier, inc=1, device_id=other_z, device_id_type=MESH)
    for c in range(4):
        state0[4 * c:4 * c + 4, :] = state_ref[c]
    pl.semaphore_wait(barrier, last + 2)

    def remote(src, dst, send_sem, recv_sem, device):
        return pltpu.make_async_remote_copy(
            src_ref=src, dst_ref=dst, send_sem=send_sem, recv_sem=recv_sem, device_id=device, device_id_type=MESH
        )

    def vel_copy(slot, device):
        return remote(vel_ref, vel_in.at[slot], vel_send_sem.at[slot], vel_recv_sem.at[slot], device)

    to_right, to_left = vel_copy(0, right), vel_copy(1, left)
    vel_y, vel_z = vel_copy(2, other_y), vel_copy(3, other_z)

    @pl.when(has_right)
    def _():
        to_right.start()

    @pl.when(has_left)
    def _():
        to_left.start()

    vel_z.start()
    vel_y.start()

    def faces(stage, state):
        ssem, rsem = face_send_sem.at[stage], face_recv_sem.at[stage]
        return (
            remote(state.at[:, NODES - LANES:], left_in.at[stage], ssem.at[0], rsem.at[0], right),
            remote(state.at[:, :LANES], right_in.at[stage], ssem.at[1], rsem.at[1], left),
            remote(state, y_in.at[stage], ssem.at[2], rsem.at[2], other_y),
            remote(state, z_in.at[stage], ssem.at[3], rsem.at[3], other_z),
        )

    def start_faces(copies):
        @pl.when(has_right)
        def _():
            copies[0].start()

        @pl.when(has_left)
        def _():
            copies[1].start()

        copies[3].start()
        copies[2].start()

    def wait_recv(copies):
        @pl.when(has_left)
        def _():
            copies[0].wait_recv()

        @pl.when(has_right)
        def _():
            copies[1].wait_recv()

        copies[2].wait_recv()
        copies[3].wait_recv()

    def wait_send(copies):
        @pl.when(has_right)
        def _():
            copies[0].wait_send()

        @pl.when(has_left)
        def _():
            copies[1].wait_send()

        copies[2].wait_send()
        copies[3].wait_send()

    faces0 = faces(0, state0)
    start_faces(faces0)

    basis = table_ref[160:168, :LANES]

    def weights(step, carry):
        for half in range(2):
            row = 2 * step + half
            position = jnp.broadcast_to(pos_ref[pl.ds(row, 1), :], (8, LANES))
            along = [
                jnp.take_along_axis(basis, index, axis=1, mode="promise_in_bounds")
                for index in (position >> 8, (position >> 4) & 15, position & 15)
            ]
            pair = along[0][:, None, :] * along[1][None, :, :]
            values = pair[:, :, None, :] * along[2][None, None, :, :]
            columns = pl.ds(pl.multiple_of(row * LANES, LANES), LANES)
            nodes[:, columns] = values.reshape(NODES, LANES).astype(jnp.bfloat16)
        return carry

    lax.fori_loop(0, 8, weights, 0)

    wait_recv((to_right, to_left, vel_y, vel_z))
    row_id = lax.broadcasted_iota(jnp.int32, (8, LANES), 0)
    lane_id = lax.broadcasted_iota(jnp.int32, (8, LANES), 1)
    sources = [[None, None] for _ in range(3)]
    own_vel = [[vel_ref[c, x].astype(f32) for x in range(2)] for c in range(3)]
    from_left = [jnp.where(has_left, vel_in[0, c, 1].astype(f32), 0.0) for c in range(3)]
    from_right = [jnp.where(has_right, vel_in[1, c, 0].astype(f32), 0.0) for c in range(3)]
    for x in range(2):
        grads, laplace = [], []
        for c in range(3):
            centre = own_vel[c][x]
            beside_y, beside_z = vel_in[2, c, x].astype(f32), vel_in[3, c, x].astype(f32)
            plus_x = own_vel[c][1] if x == 0 else from_right[c]
            minus_x = from_left[c] if x == 0 else own_vel[c][0]
            plus_y = pltpu.roll(jnp.where(row_id == 0, jnp.where(low_y, beside_y, 0.0), centre), 7, 0)
            minus_y = pltpu.roll(jnp.where(row_id == 7, jnp.where(low_y, 0.0, beside_y), centre), 1, 0)
            plus_z = pltpu.roll(jnp.where(lane_id == 0, jnp.where(low_z, beside_z, 0.0), centre), LANES - 1, 1)
            minus_z = pltpu.roll(jnp.where(lane_id == LANES - 1, jnp.where(low_z, 0.0, beside_z), centre), 1, 1)
            grads.append((0.5 * (plus_x - minus_x), 0.5 * (plus_y - minus_y), 0.5 * (plus_z - minus_z)))
            laplace.append(plus_x + minus_x + plus_y + minus_y + plus_z + minus_z - 6.0 * centre)
        curl = (
            grads[2][1] - grads[1][2],
            grads[0][2] - grads[2][0],
            grads[1][0] - grads[0][1],
        )
        for c in range(3):
            d, e = (c + 1) % 3, (c + 2) % 3
            lamb = curl[d] * own_vel[e][x] - curl[e] * own_vel[d][x]
            value = visc_ref[x] * laplace[c] - lamb
            sources[c][x] = value.astype(jnp.bfloat16).astype(f32)

    rows16 = lax.broadcasted_iota(jnp.int32, (16, LANES), 0)
    block = min(BLOCK, n)
    owner_id = lax.broadcasted_iota(jnp.int32, (block, 16, LANES), 0) * 4

    def project(first):
        pieces = []
        for x in range(2):
            for y in range(8):
                row = 8 * x + y
                segment = own_ref[row:row + 1, :] * 4 + elem_ref[row:row + 1, :] - 4 * first
                segment = jnp.broadcast_to(segment, (16, LANES)) - (rows16 & 3)
                s = [jnp.broadcast_to(sources[c][x][y:y + 1, :], (16, LANES)) for c in range(3)]
                value = jnp.where(rows16 < 4, 0.0, jnp.where(rows16 < 8, s[0], jnp.where(rows16 < 12, s[1], s[2])))
                piece = jnp.where(segment[None] == owner_id, value[None], 0.0)
                pieces.append(piece.reshape(block * 16, LANES).astype(jnp.bfloat16))
        weighted = jnp.concatenate(pieces, axis=1)
        total = lax.dot_general(
            weighted, nodes[...], (((1,), (1,)), ((), ())), preferred_element_type=f32
        ).reshape(block, 16, NODES) * MOMENT_WEIGHT
        part[pl.ds(first, block)] = total
        psend[pl.ds(first, block)] = total.astype(jnp.bfloat16)

    if n == block:
        project(0)
    else:
        lax.fori_loop(0, n // block, lambda k, c: (project(k * block), c)[1], 0)

    def part_out(k):
        to = peer(k)
        return remote(psend.at[to], precv.at[gx], part_send_sem.at[to], part_recv_sem.at[gx], {"gx": to})

    def part_into(k):
        by = peer(k)
        return remote(psend.at[by], precv.at[by], part_send_sem.at[by], part_recv_sem.at[by], {"gx": by})

    each(last, lambda k: part_out(k).start())

    lane16 = lax.broadcasted_iota(jnp.int32, (16, LANES), 1)
    b_id, c_id, e_id = (lane16 >> 3) & 7, lane16 & 7, rows16 & 3
    b_low, b_high, c_low, c_high = b_id == 0, b_id == 7, c_id == 0, c_id == 7
    on_bc = (b_low | b_high).astype(f32) + (c_low | c_high).astype(f32)
    first_half = lane16 < 64

    def tiles_of(ref):
        return [ref[:, LANES * j:LANES * (j + 1)] for j in range(TILES)]

    def local_part(x):
        top = [t[:8] for t in x]
        swapped = [pltpu.roll(t, 64, 1) for t in top]
        both = jnp.concatenate(x, axis=0)
        within = jnp.dot(
            both, table_ref[:128, :], precision=lax.Precision.HIGHEST, preferred_element_type=f32
        )
        result = []
        for j in range(TILES):
            along_a = None
            for i in range(TILES):
                at = 128 + 8 * j + 2 * i
                term = table_ref[at:at + 1, :LANES] * top[i] + table_ref[at + 1:at + 2, :LANES] * swapped[i]
                along_a = term if along_a is None else along_a + term
            faces_here = on_bc
            if j == 0:
                faces_here = on_bc + first_half.astype(f32)
            if j == TILES - 1:
                faces_here = on_bc + 1.0 - first_half.astype(f32)
            along_b = within[16 * j:16 * j + 16, :LANES]
            along_c = within[16 * j:16 * j + 16, LANES:]
            result.append((along_a, along_b, along_c, -faces_here * x[j]))
        return result

    def tendency(x, local, stage):
        result = []
        for j in range(TILES):
            columns = slice(LANES * j, LANES * (j + 1))
            along_a, along_b, along_c, faces_here = local[j]
            beside_y, beside_z = y_in[stage, :, columns], z_in[stage, :, columns]
            shifted = pltpu.roll(beside_y, jnp.where(low_y, 56, 72), 1)
            outer_b = jnp.where(jnp.where(low_y, b_id, 7 - b_id) == 7, shifted, 0.0)
            signed_b = jnp.where(low_y, outer_b, -outer_b)
            above = jnp.where(e_id == 3, jnp.where(low_z, pltpu.roll(beside_z, 3, 0), 0.0), pltpu.roll(x[j], 15, 0))
            below = jnp.where(e_id == 0, jnp.where(low_z, 0.0, pltpu.roll(beside_z, 13, 0)), pltpu.roll(x[j], 1, 0))
            upper = jnp.where(c_high, pltpu.roll(above, 7, 1), 0.0)
            lower = jnp.where(c_low, pltpu.roll(below, LANES - 7, 1), 0.0)
            outer = outer_b + upper + lower + faces_here
            if j == 0:
                outer_a = jnp.where(first_half & has_left, pltpu.roll(left_in[stage], 64, 1), 0.0)
                along_a, outer = along_a + HALF_LIFT * outer_a[:8], outer + outer_a
            if j == TILES - 1:
                outer_a = jnp.where(~first_half & has_right, pltpu.roll(right_in[stage], 64, 1), 0.0)
                along_a, outer = along_a - HALF_LIFT * outer_a[:8], outer + outer_a
            along_b = along_b - HALF_LIFT * signed_b
            along_c = along_c - HALF_LIFT * (upper - lower)
            swapped = jnp.concatenate(
                [along_a[4:8] + along_b[8:12] + along_c[12:16], along_a[0:4], along_b[0:4], along_c[0:4]], axis=0
            )
            result.append(swapped + HALF_LIFT * outer)
        return result

    start = tiles_of(state0)
    local = local_part(start)
    wait_recv(faces0)
    change = tendency(start, local, 0)
    early = [start[j] + TIME_STEP * change[j] for j in range(TILES)]

    each(last, lambda k: part_into(k).wait_recv())
    forcing = part[pl.ds(gx, 1)][0]
    if n <= 16:
        for k in range(last):
            forcing = forcing + precv[pl.ds(peer(k), 1)][0].astype(f32)
    else:
        forcing = lax.fori_loop(
            0, last, lambda k, total: total + precv[pl.ds(peer(k), 1)][0].astype(f32), forcing
        )
    push = [COUPLING * forcing[:, LANES * j:LANES * (j + 1)] for j in range(TILES)]

    one = [early[j] + TIME_STEP * push[j] for j in range(TILES)]
    for j in range(TILES):
        state1[:, LANES * j:LANES * (j + 1)] = one[j]
    faces1 = faces(1, state1)
    start_faces(faces1)
    for m in range(3):
        for e in range(4):
            mom_ref[0, 0, e, m:m + 1, :] = forcing[4 * m + 4 + e:4 * m + 5 + e, :]
    local = local_part(one)
    wait_recv(faces1)
    change = tendency(one, local, 1)
    two = [
        0.75 * start[j] + 0.25 * (one[j] + TIME_STEP * (change[j] + push[j])) for j in range(TILES)
    ]
    for j in range(TILES):
        state2[:, LANES * j:LANES * (j + 1)] = two[j]
    faces2 = faces(2, state2)
    start_faces(faces2)
    local = local_part(two)
    wait_recv(faces2)
    change = tendency(two, local, 2)
    for j in range(TILES):
        final = (1.0 / 3.0) * start[j] + (2.0 / 3.0) * (two[j] + TIME_STEP * (change[j] + push[j]))
        for c in range(4):
            next_ref[c, 0, 0, :, LANES * j:LANES * (j + 1)] = final[4 * c:4 * c + 4]

    wait_send((to_right, to_left, vel_y, vel_z))
    wait_send(faces0)
    wait_send(faces1)
    wait_send(faces2)
    each(last, lambda k: part_out(k).wait_send())


def solution(mesh):
    n = mesh.shape["gx"]
    assert mesh.shape["gy"] == 2 and mesh.shape["gz"] == 2
    f32, bf16 = jnp.float32, jnp.bfloat16
    dma = pltpu.SemaphoreType.DMA
    vmem = pl.BlockSpec(memory_space=pltpu.VMEM)

    def on_device(velocity, eddy_viscosity, cell_owner, cell_element, cell_position, acoustic_state):
        call = pl.pallas_call(
            functools.partial(kernel, n),
            out_shape=(
                jax.ShapeDtypeStruct((1, 1, 4, 3, NODES), f32),
                jax.ShapeDtypeStruct((4, 1, 1, 4, NODES), f32),
            ),
            in_specs=[vmem] * 7,
            out_specs=(vmem, vmem),
            scratch_shapes=[
                pltpu.VMEM((4, 3, 2, 8, LANES), bf16),
                pltpu.VMEM((16, NODES), f32),
                pltpu.VMEM((16, NODES), f32),
                pltpu.VMEM((16, NODES), f32),
                pltpu.VMEM((3, 16, LANES), f32),
                pltpu.VMEM((3, 16, LANES), f32),
                pltpu.VMEM((3, 16, NODES), f32),
                pltpu.VMEM((3, 16, NODES), f32),
                pltpu.VMEM((NODES, 16 * LANES), bf16),
                pltpu.VMEM((n, 16, NODES), f32),
                pltpu.VMEM((n, 16, NODES), bf16),
                pltpu.VMEM((n, 16, NODES), bf16),
                dma((4,)),
                dma((4,)),
                dma((3, 4)),
                dma((3, 4)),
                dma((n,)),
                dma((n,)),
            ],
            compiler_params=pltpu.CompilerParams(
                collective_id=0, has_side_effects=True, vmem_limit_bytes=40 * 1024 * 1024
            ),
        )
        return call(
            velocity,
            eddy_viscosity,
            cell_owner.reshape(16, LANES),
            cell_element.reshape(16, LANES),
            cell_position.reshape(16, LANES),
            acoustic_state.reshape(4, 4, NODES),
            jnp.asarray(constant_table()),
        )

    in_specs = (
        P(None, "gx", "gy", "gz"),
        P("gx", "gy", "gz"),
        P("gy", "gz", "gx", None),
        P("gy", "gz", "gx"),
        P("gy", "gz", "gx"),
        P(None, "gx", "gy", "gz", None),
    )
    out_specs = (P("gx", "gy", "gz", None, None), P(None, "gx", "gy", "gz", None))
    return jax.shard_map(on_device, mesh=mesh, in_specs=in_specs, out_specs=out_specs, check_vma=False)
```

```python
import functools

import jax
import jax.numpy as jnp
import numpy as np
from jax import lax
from jax.experimental import pallas as pl
from jax.experimental.pallas import tpu as pltpu
from jax.sharding import PartitionSpec as P

MESH = pl.DeviceIdType.MESH
SUB = 16
NODES = 512
LANES = 128
TILES = NODES // LANES
BLOCK = 8
GLL_POINTS = np.array(
    [
        -1.0,
        -0.8717401485096066,
        -0.5917001814331423,
        -0.2092992179024789,
        0.2092992179024789,
        0.5917001814331423,
        0.8717401485096066,
        1.0,
    ]
)
HALF_LIFT = 14.0
TIME_STEP = 0.01
COUPLING = 4.0
MOMENT_WEIGHT = 0.0625


def derivative_matrix():
    points = GLL_POINTS
    barycentric = np.ones(8)
    for j in range(8):
        for m in range(8):
            if m != j:
                barycentric[j] = barycentric[j] / (points[j] - points[m])
    matrix = np.zeros((8, 8))
    for i in range(8):
        for j in range(8):
            if i != j:
                matrix[i, j] = barycentric[j] / barycentric[i] / (points[i] - points[j])
        matrix[i, i] = -np.sum(matrix[i])
    return matrix


def basis_values():
    points = GLL_POINTS
    centres = -1.0 + (2.0 * np.arange(SUB) + 1.0) / SUB
    values = np.ones((SUB, 8))
    for j in range(8):
        for m in range(8):
            if m != j:
                values[:, j] = values[:, j] * (centres - points[m]) / (points[j] - points[m])
    return values


def constant_table():
    along = -derivative_matrix()
    along[0, 0] -= HALF_LIFT
    along[7, 7] += HALF_LIFT
    table = np.zeros((168, 2 * LANES))
    table[:128, :128] = np.kron(np.eye(2), np.kron(along, np.eye(8))).T
    table[:128, 128:] = np.kron(np.eye(16), along).T
    for j in range(TILES):
        for i in range(TILES):
            for h in range(2):
                lanes = slice(64 * h, 64 * h + 64)
                table[128 + 8 * j + 2 * i, lanes] = along[2 * j + h, 2 * i + h]
                table[129 + 8 * j + 2 * i, lanes] = along[2 * j + h, 2 * i + 1 - h]
    table[160:168, :SUB] = basis_values().T
    return table.astype(np.float32)


def each(count, body):
    if count <= 16:
        for k in range(count):
            body(k)
    else:
        lax.fori_loop(0, count, lambda k, c: (body(k), c)[1], 0)


def kernel(
    n,
    vel_hbm, visc_hbm, own_hbm, elem_hbm, pos_hbm, state_hbm, table_hbm,
    out_ref,
    vel_ref, visc_ref, own_ref, elem_ref, pos_ref, state_ref, table_ref, load_sem, z_out,
    vel_in, state0, state1, state2, left_in, right_in, y_in, z_in,
    nodes, part, psend, precv,
    vel_send_sem, vel_recv_sem, face_send_sem, face_recv_sem, part_send_sem, part_recv_sem,
):
    f32 = jnp.float32
    gx, gy, gz = lax.axis_index("gx"), lax.axis_index("gy"), lax.axis_index("gz")
    last = n - 1
    has_left, has_right = gx > 0, gx < last
    low_y, low_z = gy == 0, gz == 0
    left = {"gx": jnp.maximum(gx - 1, 0)}
    right = {"gx": jnp.minimum(gx + 1, last)}
    other_y, other_z = {"gy": 1 - gy}, {"gz": 1 - gz}

    def peer(k):
        return lax.rem(gx + 1 + k, n)

    barrier = pltpu.get_barrier_semaphore()
    each(last, lambda k: pl.semaphore_signal(barrier, inc=1, device_id={"gx": peer(k)}, device_id_type=MESH))
    pl.semaphore_signal(barrier, inc=1, device_id=other_y, device_id_type=MESH)
    pl.semaphore_signal(barrier, inc=1, device_id=other_z, device_id_type=MESH)
    loads = [
        pltpu.make_async_copy(src, dst, load_sem.at[k])
        for k, (src, dst) in enumerate(
            (
                (vel_hbm, vel_ref), (pos_hbm, pos_ref), (table_hbm, table_ref), (state_hbm, state_ref),
                (own_hbm, own_ref), (elem_hbm, elem_ref), (visc_hbm, visc_ref),
            )
        )
    ]
    for load in loads:
        load.start()
    pl.semaphore_wait(barrier, last + 2)

    def remote(src, dst, send_sem, recv_sem, device):
        return pltpu.make_async_remote_copy(
            src_ref=src, dst_ref=dst, send_sem=send_sem, recv_sem=recv_sem, device_id=device, device_id_type=MESH
        )

    def vel_copy(slot, device):
        return remote(vel_hbm, vel_in.at[slot], vel_send_sem.at[slot], vel_recv_sem.at[slot], device)

    to_right, to_left = vel_copy(0, right), vel_copy(1, left)
    vel_y, vel_z = vel_copy(2, other_y), vel_copy(3, other_z)

    @pl.when(has_right)
    def _():
        to_right.start()

    @pl.when(has_left)
    def _():
        to_left.start()

    vel_z.start()
    vel_y.start()

    def faces(stage, state):
        ssem, rsem = face_send_sem.at[stage], face_recv_sem.at[stage]
        return (
            remote(state.at[:, NODES - LANES:], left_in.at[stage], ssem.at[0], rsem.at[0], right),
            remote(state.at[:, :LANES], right_in.at[stage], ssem.at[1], rsem.at[1], left),
            remote(state, y_in.at[stage], ssem.at[2], rsem.at[2], other_y),
            remote(z_out.at[stage], z_in.at[stage], ssem.at[3], rsem.at[3], other_z),
        )

    def start_faces(copies):
        @pl.when(has_right)
        def _():
            copies[0].start()

        @pl.when(has_left)
        def _():
            copies[1].start()

        copies[3].start()
        copies[2].start()

    def wait_recv(copies):
        @pl.when(has_left)
        def _():
            copies[0].wait_recv()

        @pl.when(has_right)
        def _():
            copies[1].wait_recv()

        copies[2].wait_recv()
        copies[3].wait_recv()

    def wait_send(copies):
        @pl.when(has_right)
        def _():
            copies[0].wait_send()

        @pl.when(has_left)
        def _():
            copies[1].wait_send()

        copies[2].wait_send()
        copies[3].wait_send()

    row_id = lax.broadcasted_iota(jnp.int32, (8, LANES), 0)
    lane_id = lax.broadcasted_iota(jnp.int32, (8, LANES), 1)
    rows16 = lax.broadcasted_iota(jnp.int32, (16, LANES), 0)
    lane16 = lax.broadcasted_iota(jnp.int32, (16, LANES), 1)
    b_id, c_id, e_id = (lane16 >> 3) & 7, lane16 & 7, rows16 & 3

    def tiles_of(ref):
        return [ref[:, LANES * j:LANES * (j + 1)] for j in range(TILES)]

    def pack_z(x, stage):
        packed = x[0]
        for j in range(TILES):
            shift = jnp.where(low_z, (j - 7) % LANES, j)
            packed = jnp.where(c_id == j, pltpu.roll(x[j], shift, 1), packed)
        z_out[stage] = packed

    loads[3].wait()
    for c in range(4):
        state0[4 * c:4 * c + 4, :] = state_ref[c]
    start = tiles_of(state0)
    pack_z(start, 0)
    faces0 = faces(0, state0)
    start_faces(faces0)
    loads[1].wait()
    loads[2].wait()

    basis = table_ref[160:168, :LANES]

    def weights(step, carry):
        for half in range(2):
            row = 2 * step + half
            position = jnp.broadcast_to(pos_ref[pl.ds(row, 1), :], (8, LANES))
            along = [
                jnp.take_along_axis(basis, index, axis=1, mode="promise_in_bounds")
                for index in (position >> 8, (position >> 4) & 15, position & 15)
            ]
            pair = along[0][:, None, :] * along[1][None, :, :]
            values = pair[:, :, None, :] * along[2][None, None, :, :]
            columns = pl.ds(pl.multiple_of(row * LANES, LANES), LANES)
            nodes[:, columns] = values.reshape(NODES, LANES).astype(jnp.bfloat16)
        return carry

    lax.fori_loop(0, 8, weights, 0)

    loads[0].wait()
    for load in loads[4:]:
        load.wait()
    wait_recv((to_right, to_left, vel_y, vel_z))
    sources = [[None, None] for _ in range(3)]
    own_vel = [[vel_ref[c, x].astype(f32) for x in range(2)] for c in range(3)]
    from_left = [jnp.where(has_left, vel_in[0, c, 1].astype(f32), 0.0) for c in range(3)]
    from_right = [jnp.where(has_right, vel_in[1, c, 0].astype(f32), 0.0) for c in range(3)]
    for x in range(2):
        grads, laplace = [], []
        for c in range(3):
            centre = own_vel[c][x]
            beside_y, beside_z = vel_in[2, c, x].astype(f32), vel_in[3, c, x].astype(f32)
            plus_x = own_vel[c][1] if x == 0 else from_right[c]
            minus_x = from_left[c] if x == 0 else own_vel[c][0]
            plus_y = pltpu.roll(jnp.where(row_id == 0, jnp.where(low_y, beside_y, 0.0), centre), 7, 0)
            minus_y = pltpu.roll(jnp.where(row_id == 7, jnp.where(low_y, 0.0, beside_y), centre), 1, 0)
            plus_z = pltpu.roll(jnp.where(lane_id == 0, jnp.where(low_z, beside_z, 0.0), centre), LANES - 1, 1)
            minus_z = pltpu.roll(jnp.where(lane_id == LANES - 1, jnp.where(low_z, 0.0, beside_z), centre), 1, 1)
            grads.append((0.5 * (plus_x - minus_x), 0.5 * (plus_y - minus_y), 0.5 * (plus_z - minus_z)))
            laplace.append(plus_x + minus_x + plus_y + minus_y + plus_z + minus_z - 6.0 * centre)
        curl = (
            grads[2][1] - grads[1][2],
            grads[0][2] - grads[2][0],
            grads[1][0] - grads[0][1],
        )
        for c in range(3):
            d, e = (c + 1) % 3, (c + 2) % 3
            lamb = curl[d] * own_vel[e][x] - curl[e] * own_vel[d][x]
            value = visc_ref[x] * laplace[c] - lamb
            sources[c][x] = value.astype(jnp.bfloat16).astype(f32)

    block = min(BLOCK, n)
    owner_id = lax.broadcasted_iota(jnp.int32, (block, 16, LANES), 0) * 4

    def project(first):
        pieces = []
        for x in range(2):
            for y in range(8):
                row = 8 * x + y
                segment = own_ref[row:row + 1, :] * 4 + elem_ref[row:row + 1, :] - 4 * first
                segment = jnp.broadcast_to(segment, (16, LANES)) - (rows16 & 3)
                s = [jnp.broadcast_to(sources[c][x][y:y + 1, :], (16, LANES)) for c in range(3)]
                value = jnp.where(rows16 < 4, 0.0, jnp.where(rows16 < 8, s[0], jnp.where(rows16 < 12, s[1], s[2])))
                piece = jnp.where(segment[None] == owner_id, value[None], 0.0)
                pieces.append(piece.reshape(block * 16, LANES).astype(jnp.bfloat16))
        weighted = jnp.concatenate(pieces, axis=1)
        total = lax.dot_general(
            weighted, nodes[...], (((1,), (1,)), ((), ())), preferred_element_type=f32
        ).reshape(block, 16, NODES) * MOMENT_WEIGHT
        packed = jnp.concatenate(
            [
                jnp.concatenate(
                    [total[:, 4 * m + 4:4 * m + 8, LANES * j:LANES * (j + 1)] for j in range(TILES)], axis=1
                )
                for m in range(3)
            ],
            axis=2,
        )
        part[pl.ds(first, block)] = packed
        psend[pl.ds(first, block)] = packed.astype(jnp.bfloat16)

    if n == block:
        project(0)
    else:
        lax.fori_loop(0, n // block, lambda k, c: (project(k * block), c)[1], 0)

    def part_out(k):
        to = peer(k)
        return remote(psend.at[to], precv.at[gx], part_send_sem.at[to], part_recv_sem.at[gx], {"gx": to})

    def part_into(k):
        by = peer(k)
        return remote(psend.at[by], precv.at[by], part_send_sem.at[by], part_recv_sem.at[by], {"gx": by})

    each(last, lambda k: part_out(k).start())

    b_low, b_high, c_low, c_high = b_id == 0, b_id == 7, c_id == 0, c_id == 7
    on_bc = (b_low | b_high).astype(f32) + (c_low | c_high).astype(f32)
    first_half = lane16 < 64
    on_z = jnp.where(low_z, c_id + e_id, 10 - c_id - e_id) == 10

    def local_part(x):
        top = [t[:8] for t in x]
        swapped = [pltpu.roll(t, 64, 1) for t in top]
        both = jnp.concatenate(x, axis=0)
        within = jnp.dot(
            both, table_ref[:128, :], precision=lax.Precision.HIGHEST, preferred_element_type=f32
        )
        result = []
        for j in range(TILES):
            along_a = None
            for i in range(TILES):
                at = 128 + 8 * j + 2 * i
                term = table_ref[at:at + 1, :LANES] * top[i] + table_ref[at + 1:at + 2, :LANES] * swapped[i]
                along_a = term if along_a is None else along_a + term
            faces_here = on_bc
            if j == 0:
                faces_here = on_bc + first_half.astype(f32)
            if j == TILES - 1:
                faces_here = on_bc + 1.0 - first_half.astype(f32)
            along_b = within[16 * j:16 * j + 16, :LANES]
            along_c = within[16 * j:16 * j + 16, LANES:]
            above = jnp.where(e_id == 3, 0.0, pltpu.roll(x[j], 15, 0))
            below = jnp.where(e_id == 0, 0.0, pltpu.roll(x[j], 1, 0))
            upper = jnp.where(c_high, pltpu.roll(above, 7, 1), 0.0)
            lower = jnp.where(c_low, pltpu.roll(below, LANES - 7, 1), 0.0)
            along_c = along_c - HALF_LIFT * (upper - lower)
            result.append((along_a, along_b, along_c, upper + lower - faces_here * x[j]))
        return result

    def tendency(local, stage):
        result = []
        beside_z = pltpu.roll(z_in[stage], jnp.where(low_z, 3, 13), 0)
        for j in range(TILES):
            columns = slice(LANES * j, LANES * (j + 1))
            along_a, along_b, along_c, faces_here = local[j]
            beside_y = y_in[stage, :, columns]
            shifted = pltpu.roll(beside_y, jnp.where(low_y, 56, 72), 1)
            outer_b = jnp.where(jnp.where(low_y, b_id, 7 - b_id) == 7, shifted, 0.0)
            signed_b = jnp.where(low_y, outer_b, -outer_b)
            outer_c = jnp.where(on_z, pltpu.roll(beside_z, jnp.where(low_z, 7 - j, (LANES - j) % LANES), 1), 0.0)
            outer = outer_b + outer_c + faces_here
            if j == 0:
                outer_a = jnp.where(first_half & has_left, pltpu.roll(left_in[stage], 64, 1), 0.0)
                along_a, outer = along_a + HALF_LIFT * outer_a[:8], outer + outer_a
            if j == TILES - 1:
                outer_a = jnp.where(~first_half & has_right, pltpu.roll(right_in[stage], 64, 1), 0.0)
                along_a, outer = along_a - HALF_LIFT * outer_a[:8], outer + outer_a
            along_b = along_b - HALF_LIFT * signed_b
            along_c = along_c - HALF_LIFT * jnp.where(low_z, outer_c, -outer_c)
            swapped = jnp.concatenate(
                [along_a[4:8] + along_b[8:12] + along_c[12:16], along_a[0:4], along_b[0:4], along_c[0:4]], axis=0
            )
            result.append(swapped + HALF_LIFT * outer)
        return result

    local = local_part(start)
    wait_recv(faces0)
    change = tendency(local, 0)
    early = [start[j] + TIME_STEP * change[j] for j in range(TILES)]

    each(last, lambda k: part_into(k).wait_recv())
    forcing = part[pl.ds(gx, 1)][0]
    if n <= 16:
        for k in range(last):
            forcing = forcing + precv[pl.ds(peer(k), 1)][0].astype(f32)
    else:
        forcing = lax.fori_loop(
            0, last, lambda k, total: total + precv[pl.ds(peer(k), 1)][0].astype(f32), forcing
        )
    moments = [
        [forcing[4 * j:4 * j + 4, LANES * m:LANES * (m + 1)] for m in range(3)] for j in range(TILES)
    ]
    none = jnp.zeros((4, LANES), f32)
    push = [COUPLING * jnp.concatenate([none] + moments[j], axis=0) for j in range(TILES)]

    one = [early[j] + TIME_STEP * push[j] for j in range(TILES)]
    for j in range(TILES):
        state1[:, LANES * j:LANES * (j + 1)] = one[j]
    pack_z(one, 1)
    faces1 = faces(1, state1)
    start_faces(faces1)
    for m in range(3):
        for j in range(TILES):
            out_ref[4 + m, :, LANES * j:LANES * (j + 1)] = moments[j][m]
    local = local_part(one)
    wait_recv(faces1)
    change = tendency(local, 1)
    two = [
        0.75 * start[j] + 0.25 * (one[j] + TIME_STEP * (change[j] + push[j])) for j in range(TILES)
    ]
    for j in range(TILES):
        state2[:, LANES * j:LANES * (j + 1)] = two[j]
    pack_z(two, 2)
    faces2 = faces(2, state2)
    start_faces(faces2)
    local = local_part(two)
    wait_recv(faces2)
    change = tendency(local, 2)
    for j in range(TILES):
        final = (1.0 / 3.0) * start[j] + (2.0 / 3.0) * (two[j] + TIME_STEP * (change[j] + push[j]))
        for c in range(4):
            out_ref[c, :, LANES * j:LANES * (j + 1)] = final[4 * c:4 * c + 4]

    wait_send((to_right, to_left, vel_y, vel_z))
    wait_send(faces0)
    wait_send(faces1)
    wait_send(faces2)
    each(last, lambda k: part_out(k).wait_send())


def solution(mesh):
    n = mesh.shape["gx"]
    assert mesh.shape["gy"] == 2 and mesh.shape["gz"] == 2
    f32, bf16 = jnp.float32, jnp.bfloat16
    dma = pltpu.SemaphoreType.DMA

    def on_device(velocity, eddy_viscosity, cell_owner, cell_element, cell_position, acoustic_state):
        call = pl.pallas_call(
            functools.partial(kernel, n),
            out_shape=jax.ShapeDtypeStruct((7, 4, NODES), f32),
            in_specs=[pl.BlockSpec(memory_space=pltpu.HBM)] * 7,
            out_specs=pl.BlockSpec(memory_space=pltpu.VMEM),
            scratch_shapes=[
                pltpu.VMEM((3, 2, 8, LANES), bf16),
                pltpu.VMEM((2, 8, LANES), f32),
                pltpu.VMEM((16, LANES), jnp.int32),
                pltpu.VMEM((16, LANES), jnp.int32),
                pltpu.VMEM((16, LANES), jnp.int32),
                pltpu.VMEM((4, 4, NODES), f32),
                pltpu.VMEM((168, 2 * LANES), f32),
                dma((7,)),
                pltpu.VMEM((3, 16, LANES), f32),
                pltpu.VMEM((4, 3, 2, 8, LANES), bf16),
                pltpu.VMEM((16, NODES), f32),
                pltpu.VMEM((16, NODES), f32),
                pltpu.VMEM((16, NODES), f32),
                pltpu.VMEM((3, 16, LANES), f32),
                pltpu.VMEM((3, 16, LANES), f32),
                pltpu.VMEM((3, 16, NODES), f32),
                pltpu.VMEM((3, 16, LANES), f32),
                pltpu.VMEM((NODES, 16 * LANES), bf16),
                pltpu.VMEM((n, 16, 3 * LANES), f32),
                pltpu.VMEM((n, 16, 3 * LANES), bf16),
                pltpu.VMEM((n, 16, 3 * LANES), bf16),
                dma((4,)),
                dma((4,)),
                dma((3, 4)),
                dma((3, 4)),
                dma((n,)),
                dma((n,)),
            ],
            compiler_params=pltpu.CompilerParams(
                collective_id=0, has_side_effects=True, vmem_limit_bytes=63 * 1024 * 1024
            ),
        )
        out = call(
            velocity,
            eddy_viscosity,
            cell_owner.reshape(16, LANES),
            cell_element.reshape(16, LANES),
            cell_position.reshape(16, LANES),
            acoustic_state.reshape(4, 4, NODES),
            jnp.asarray(constant_table()),
        )
        moments = jnp.transpose(out[4:], (1, 0, 2)).reshape(1, 1, 4, 3, NODES)
        return moments, out[:4].reshape(4, 1, 1, 4, NODES)

    in_specs = (
        P(None, "gx", "gy", "gz"),
        P("gx", "gy", "gz"),
        P("gy", "gz", "gx", None),
        P("gy", "gz", "gx"),
        P("gy", "gz", "gx"),
        P(None, "gx", "gy", "gz", None),
    )
    out_specs = (P("gx", "gy", "gz", None, None), P(None, "gx", "gy", "gz", None))
    return jax.shard_map(on_device, mesh=mesh, in_specs=in_specs, out_specs=out_specs, check_vma=False)
```

```python
import functools

import jax
import jax.numpy as jnp
import numpy as np
from jax import lax
from jax.experimental import pallas as pl
from jax.experimental.pallas import tpu as pltpu
from jax.sharding import PartitionSpec as P

MESH = pl.DeviceIdType.MESH
SUB = 16
NODES = 512
LANES = 128
TILES = NODES // LANES
BLOCK = 8
GLL_POINTS = np.array(
    [
        -1.0,
        -0.8717401485096066,
        -0.5917001814331423,
        -0.2092992179024789,
        0.2092992179024789,
        0.5917001814331423,
        0.8717401485096066,
        1.0,
    ]
)
HALF_LIFT = 14.0
TIME_STEP = 0.01
COUPLING = 4.0
MOMENT_WEIGHT = 0.0625


def derivative_matrix():
    points = GLL_POINTS
    barycentric = np.ones(8)
    for j in range(8):
        for m in range(8):
            if m != j:
                barycentric[j] = barycentric[j] / (points[j] - points[m])
    matrix = np.zeros((8, 8))
    for i in range(8):
        for j in range(8):
            if i != j:
                matrix[i, j] = barycentric[j] / barycentric[i] / (points[i] - points[j])
        matrix[i, i] = -np.sum(matrix[i])
    return matrix


def basis_values():
    points = GLL_POINTS
    centres = -1.0 + (2.0 * np.arange(SUB) + 1.0) / SUB
    values = np.ones((SUB, 8))
    for j in range(8):
        for m in range(8):
            if m != j:
                values[:, j] = values[:, j] * (centres - points[m]) / (points[j] - points[m])
    return values


def constant_table():
    along = -derivative_matrix()
    along[0, 0] -= HALF_LIFT
    along[7, 7] += HALF_LIFT
    table = np.zeros((168, 2 * LANES))
    table[:128, :128] = np.kron(np.eye(2), np.kron(along, np.eye(8))).T
    table[:128, 128:] = np.kron(np.eye(16), along).T
    for j in range(TILES):
        for i in range(TILES):
            for h in range(2):
                lanes = slice(64 * h, 64 * h + 64)
                table[128 + 8 * j + 2 * i, lanes] = along[2 * j + h, 2 * i + h]
                table[129 + 8 * j + 2 * i, lanes] = along[2 * j + h, 2 * i + 1 - h]
    table[160:168, :SUB] = basis_values().T
    return table.astype(np.float32)


def each(count, body):
    if count <= 16:
        for k in range(count):
            body(k)
    else:
        lax.fori_loop(0, count, lambda k, c: (body(k), c)[1], 0)


def kernel(
    n,
    vel_hbm, visc_hbm, own_hbm, elem_hbm, pos_hbm, state_hbm, table_hbm,
    out_ref,
    vel_ref, visc_ref, own_ref, elem_ref, pos_ref, state_ref, table_ref, load_sem, z_out,
    vel_in, state0, state1, state2, left_in, right_in, y_in, z_in,
    nodes, part, psend, precv,
    vel_send_sem, vel_recv_sem, face_send_sem, face_recv_sem, part_send_sem, part_recv_sem,
):
    f32 = jnp.float32
    gx, gy, gz = lax.axis_index("gx"), lax.axis_index("gy"), lax.axis_index("gz")
    last = n - 1
    has_left, has_right = gx > 0, gx < last
    low_y, low_z = gy == 0, gz == 0
    left = {"gx": jnp.maximum(gx - 1, 0)}
    right = {"gx": jnp.minimum(gx + 1, last)}
    other_y, other_z = {"gy": 1 - gy}, {"gz": 1 - gz}

    def peer(k):
        return lax.rem(gx + 1 + k, n)

    barrier = pltpu.get_barrier_semaphore()
    each(last, lambda k: pl.semaphore_signal(barrier, inc=1, device_id={"gx": peer(k)}, device_id_type=MESH))
    pl.semaphore_signal(barrier, inc=1, device_id=other_y, device_id_type=MESH)
    pl.semaphore_signal(barrier, inc=1, device_id=other_z, device_id_type=MESH)
    loads = [
        pltpu.make_async_copy(src, dst, load_sem.at[k])
        for k, (src, dst) in enumerate(
            (
                (vel_hbm, vel_ref), (pos_hbm, pos_ref), (table_hbm, table_ref), (state_hbm, state_ref),
                (own_hbm, own_ref), (elem_hbm, elem_ref), (visc_hbm, visc_ref),
            )
        )
    ]
    for load in loads:
        load.start()
    pl.semaphore_wait(barrier, last + 2)

    def remote(src, dst, send_sem, recv_sem, device):
        return pltpu.make_async_remote_copy(
            src_ref=src, dst_ref=dst, send_sem=send_sem, recv_sem=recv_sem, device_id=device, device_id_type=MESH
        )

    def vel_copy(slot, device):
        return remote(vel_hbm, vel_in.at[slot], vel_send_sem.at[slot], vel_recv_sem.at[slot], device)

    to_right, to_left = vel_copy(0, right), vel_copy(1, left)
    vel_y, vel_z = vel_copy(2, other_y), vel_copy(3, other_z)

    @pl.when(has_right)
    def _():
        to_right.start()

    @pl.when(has_left)
    def _():
        to_left.start()

    vel_z.start()
    vel_y.start()

    def faces(stage, state):
        ssem, rsem = face_send_sem.at[stage], face_recv_sem.at[stage]
        return (
            remote(state.at[:, NODES - LANES:], left_in.at[stage], ssem.at[0], rsem.at[0], right),
            remote(state.at[:, :LANES], right_in.at[stage], ssem.at[1], rsem.at[1], left),
            remote(state, y_in.at[stage], ssem.at[2], rsem.at[2], other_y),
            remote(z_out.at[stage], z_in.at[stage], ssem.at[3], rsem.at[3], other_z),
        )

    def start_faces(copies):
        @pl.when(has_right)
        def _():
            copies[0].start()

        @pl.when(has_left)
        def _():
            copies[1].start()

        copies[3].start()
        copies[2].start()

    def wait_recv(copies):
        @pl.when(has_left)
        def _():
            copies[0].wait_recv()

        @pl.when(has_right)
        def _():
            copies[1].wait_recv()

        copies[2].wait_recv()
        copies[3].wait_recv()

    def wait_send(copies):
        @pl.when(has_right)
        def _():
            copies[0].wait_send()

        @pl.when(has_left)
        def _():
            copies[1].wait_send()

        copies[2].wait_send()
        copies[3].wait_send()

    row_id = lax.broadcasted_iota(jnp.int32, (8, LANES), 0)
    lane_id = lax.broadcasted_iota(jnp.int32, (8, LANES), 1)
    rows16 = lax.broadcasted_iota(jnp.int32, (16, LANES), 0)
    lane16 = lax.broadcasted_iota(jnp.int32, (16, LANES), 1)
    b_id, c_id, e_id = (lane16 >> 3) & 7, lane16 & 7, rows16 & 3

    def tiles_of(ref):
        return [ref[:, LANES * j:LANES * (j + 1)] for j in range(TILES)]

    def pack_z(x, stage):
        packed = x[0]
        for j in range(TILES):
            shift = jnp.where(low_z, (j - 7) % LANES, j)
            packed = jnp.where(c_id == j, pltpu.roll(x[j], shift, 1), packed)
        z_out[stage] = packed

    loads[1].wait()
    loads[2].wait()

    basis = table_ref[160:168, :LANES]

    def weights(step, carry):
        for half in range(2):
            row = 2 * step + half
            position = jnp.broadcast_to(pos_ref[pl.ds(row, 1), :], (8, LANES))
            along = [
                jnp.take_along_axis(basis, index, axis=1, mode="promise_in_bounds")
                for index in (position >> 8, (position >> 4) & 15, position & 15)
            ]
            pair = along[0][:, None, :] * along[1][None, :, :]
            values = pair[:, :, None, :] * along[2][None, None, :, :]
            columns = pl.ds(pl.multiple_of(row * LANES, LANES), LANES)
            nodes[:, columns] = values.reshape(NODES, LANES).astype(jnp.bfloat16)
        return carry

    lax.fori_loop(0, 8, weights, 0)

    loads[3].wait()
    for c in range(4):
        state0[4 * c:4 * c + 4, :] = state_ref[c]
    start = tiles_of(state0)
    pack_z(start, 0)
    faces0 = faces(0, state0)
    start_faces(faces0)
    loads[0].wait()
    for load in loads[4:]:
        load.wait()
    wait_recv((to_right, to_left, vel_y, vel_z))
    sources = [[None, None] for _ in range(3)]
    own_vel = [[vel_ref[c, x].astype(f32) for x in range(2)] for c in range(3)]
    from_left = [jnp.where(has_left, vel_in[0, c, 1].astype(f32), 0.0) for c in range(3)]
    from_right = [jnp.where(has_right, vel_in[1, c, 0].astype(f32), 0.0) for c in range(3)]
    for x in range(2):
        grads, laplace = [], []
        for c in range(3):
            centre = own_vel[c][x]
            beside_y, beside_z = vel_in[2, c, x].astype(f32), vel_in[3, c, x].astype(f32)
            plus_x = own_vel[c][1] if x == 0 else from_right[c]
            minus_x = from_left[c] if x == 0 else own_vel[c][0]
            plus_y = pltpu.roll(jnp.where(row_id == 0, jnp.where(low_y, beside_y, 0.0), centre), 7, 0)
            minus_y = pltpu.roll(jnp.where(row_id == 7, jnp.where(low_y, 0.0, beside_y), centre), 1, 0)
            plus_z = pltpu.roll(jnp.where(lane_id == 0, jnp.where(low_z, beside_z, 0.0), centre), LANES - 1, 1)
            minus_z = pltpu.roll(jnp.where(lane_id == LANES - 1, jnp.where(low_z, 0.0, beside_z), centre), 1, 1)
            grads.append((0.5 * (plus_x - minus_x), 0.5 * (plus_y - minus_y), 0.5 * (plus_z - minus_z)))
            laplace.append(plus_x + minus_x + plus_y + minus_y + plus_z + minus_z - 6.0 * centre)
        curl = (
            grads[2][1] - grads[1][2],
            grads[0][2] - grads[2][0],
            grads[1][0] - grads[0][1],
        )
        for c in range(3):
            d, e = (c + 1) % 3, (c + 2) % 3
            lamb = curl[d] * own_vel[e][x] - curl[e] * own_vel[d][x]
            value = visc_ref[x] * laplace[c] - lamb
            sources[c][x] = value.astype(jnp.bfloat16).astype(f32)

    block = min(BLOCK, n)
    owner_id = lax.broadcasted_iota(jnp.int32, (block, 16, LANES), 0) * 4

    def project(first):
        pieces = []
        for x in range(2):
            for y in range(8):
                row = 8 * x + y
                segment = own_ref[row:row + 1, :] * 4 + elem_ref[row:row + 1, :] - 4 * first
                segment = jnp.broadcast_to(segment, (16, LANES)) - (rows16 & 3)
                s = [jnp.broadcast_to(sources[c][x][y:y + 1, :], (16, LANES)) for c in range(3)]
                value = jnp.where(rows16 < 4, 0.0, jnp.where(rows16 < 8, s[0], jnp.where(rows16 < 12, s[1], s[2])))
                piece = jnp.where(segment[None] == owner_id, value[None], 0.0)
                pieces.append(piece.reshape(block * 16, LANES).astype(jnp.bfloat16))
        weighted = jnp.concatenate(pieces, axis=1)
        total = lax.dot_general(
            weighted, nodes[...], (((1,), (1,)), ((), ())), preferred_element_type=f32
        ).reshape(block, 16, NODES) * MOMENT_WEIGHT
        packed = jnp.concatenate(
            [
                jnp.concatenate(
                    [total[:, 4 * m + 4:4 * m + 8, LANES * j:LANES * (j + 1)] for j in range(TILES)], axis=1
                )
                for m in range(3)
            ],
            axis=2,
        )
        part[pl.ds(first, block)] = packed
        psend[pl.ds(first, block)] = packed.astype(jnp.bfloat16)

    if n == block:
        project(0)
    else:
        lax.fori_loop(0, n // block, lambda k, c: (project(k * block), c)[1], 0)

    def part_out(k):
        to = peer(k)
        return remote(psend.at[to], precv.at[gx], part_send_sem.at[to], part_recv_sem.at[gx], {"gx": to})

    def part_into(k):
        by = peer(k)
        return remote(psend.at[by], precv.at[by], part_send_sem.at[by], part_recv_sem.at[by], {"gx": by})

    each(last, lambda k: part_out(k).start())

    b_low, b_high, c_low, c_high = b_id == 0, b_id == 7, c_id == 0, c_id == 7
    on_bc = (b_low | b_high).astype(f32) + (c_low | c_high).astype(f32)
    first_half = lane16 < 64
    on_z = jnp.where(low_z, c_id + e_id, 10 - c_id - e_id) == 10

    def local_part(x):
        top = [t[:8] for t in x]
        swapped = [pltpu.roll(t, 64, 1) for t in top]
        both = jnp.concatenate(x, axis=0)
        within = jnp.dot(
            both, table_ref[:128, :], precision=lax.Precision.HIGHEST, preferred_element_type=f32
        )
        result = []
        for j in range(TILES):
            along_a = None
            for i in range(TILES):
                at = 128 + 8 * j + 2 * i
                term = table_ref[at:at + 1, :LANES] * top[i] + table_ref[at + 1:at + 2, :LANES] * swapped[i]
                along_a = term if along_a is None else along_a + term
            faces_here = on_bc
            if j == 0:
                faces_here = on_bc + first_half.astype(f32)
            if j == TILES - 1:
                faces_here = on_bc + 1.0 - first_half.astype(f32)
            along_b = within[16 * j:16 * j + 16, :LANES]
            along_c = within[16 * j:16 * j + 16, LANES:]
            above = jnp.where(e_id == 3, 0.0, pltpu.roll(x[j], 15, 0))
            below = jnp.where(e_id == 0, 0.0, pltpu.roll(x[j], 1, 0))
            upper = jnp.where(c_high, pltpu.roll(above, 7, 1), 0.0)
            lower = jnp.where(c_low, pltpu.roll(below, LANES - 7, 1), 0.0)
            along_c = along_c - HALF_LIFT * (upper - lower)
            result.append((along_a, along_b, along_c, upper + lower - faces_here * x[j]))
        return result

    def tendency(local, stage):
        result = []
        beside_z = pltpu.roll(z_in[stage], jnp.where(low_z, 3, 13), 0)
        for j in range(TILES):
            columns = slice(LANES * j, LANES * (j + 1))
            along_a, along_b, along_c, faces_here = local[j]
            beside_y = y_in[stage, :, columns]
            shifted = pltpu.roll(beside_y, jnp.where(low_y, 56, 72), 1)
            outer_b = jnp.where(jnp.where(low_y, b_id, 7 - b_id) == 7, shifted, 0.0)
            signed_b = jnp.where(low_y, outer_b, -outer_b)
            outer_c = jnp.where(on_z, pltpu.roll(beside_z, jnp.where(low_z, 7 - j, (LANES - j) % LANES), 1), 0.0)
            outer = outer_b + outer_c + faces_here
            if j == 0:
                outer_a = jnp.where(first_half & has_left, pltpu.roll(left_in[stage], 64, 1), 0.0)
                along_a, outer = along_a + HALF_LIFT * outer_a[:8], outer + outer_a
            if j == TILES - 1:
                outer_a = jnp.where(~first_half & has_right, pltpu.roll(right_in[stage], 64, 1), 0.0)
                along_a, outer = along_a - HALF_LIFT * outer_a[:8], outer + outer_a
            along_b = along_b - HALF_LIFT * signed_b
            along_c = along_c - HALF_LIFT * jnp.where(low_z, outer_c, -outer_c)
            swapped = jnp.concatenate(
                [along_a[4:8] + along_b[8:12] + along_c[12:16], along_a[0:4], along_b[0:4], along_c[0:4]], axis=0
            )
            result.append(swapped + HALF_LIFT * outer)
        return result

    local = local_part(start)
    wait_recv(faces0)
    change = tendency(local, 0)
    early = [start[j] + TIME_STEP * change[j] for j in range(TILES)]

    each(last, lambda k: part_into(k).wait_recv())
    forcing = part[pl.ds(gx, 1)][0]
    if n <= 16:
        for k in range(last):
            forcing = forcing + precv[pl.ds(peer(k), 1)][0].astype(f32)
    else:
        forcing = lax.fori_loop(
            0, last, lambda k, total: total + precv[pl.ds(peer(k), 1)][0].astype(f32), forcing
        )
    moments = [
        [forcing[4 * j:4 * j + 4, LANES * m:LANES * (m + 1)] for m in range(3)] for j in range(TILES)
    ]
    none = jnp.zeros((4, LANES), f32)
    push = [COUPLING * jnp.concatenate([none] + moments[j], axis=0) for j in range(TILES)]

    one = [early[j] + TIME_STEP * push[j] for j in range(TILES)]
    for j in range(TILES):
        state1[:, LANES * j:LANES * (j + 1)] = one[j]
    pack_z(one, 1)
    faces1 = faces(1, state1)
    start_faces(faces1)
    for m in range(3):
        for j in range(TILES):
            out_ref[4 + m, :, LANES * j:LANES * (j + 1)] = moments[j][m]
    local = local_part(one)
    wait_recv(faces1)
    change = tendency(local, 1)
    two = [
        0.75 * start[j] + 0.25 * (one[j] + TIME_STEP * (change[j] + push[j])) for j in range(TILES)
    ]
    for j in range(TILES):
        state2[:, LANES * j:LANES * (j + 1)] = two[j]
    pack_z(two, 2)
    faces2 = faces(2, state2)
    start_faces(faces2)
    local = local_part(two)
    wait_recv(faces2)
    change = tendency(local, 2)
    for j in range(TILES):
        final = (1.0 / 3.0) * start[j] + (2.0 / 3.0) * (two[j] + TIME_STEP * (change[j] + push[j]))
        for c in range(4):
            out_ref[c, :, LANES * j:LANES * (j + 1)] = final[4 * c:4 * c + 4]

    wait_send((to_right, to_left, vel_y, vel_z))
    wait_send(faces0)
    wait_send(faces1)
    wait_send(faces2)
    each(last, lambda k: part_out(k).wait_send())


def solution(mesh):
    n = mesh.shape["gx"]
    assert mesh.shape["gy"] == 2 and mesh.shape["gz"] == 2
    f32, bf16 = jnp.float32, jnp.bfloat16
    dma = pltpu.SemaphoreType.DMA

    def on_device(velocity, eddy_viscosity, cell_owner, cell_element, cell_position, acoustic_state):
        call = pl.pallas_call(
            functools.partial(kernel, n),
            out_shape=pltpu.VMEM((7, 4, NODES), f32),
            in_specs=[pl.BlockSpec(memory_space=pltpu.HBM)] * 7,
            out_specs=pl.BlockSpec(memory_space=pltpu.VMEM),
            scratch_shapes=[
                pltpu.VMEM((3, 2, 8, LANES), bf16),
                pltpu.VMEM((2, 8, LANES), f32),
                pltpu.VMEM((16, LANES), jnp.int32),
                pltpu.VMEM((16, LANES), jnp.int32),
                pltpu.VMEM((16, LANES), jnp.int32),
                pltpu.VMEM((4, 4, NODES), f32),
                pltpu.VMEM((168, 2 * LANES), f32),
                dma((7,)),
                pltpu.VMEM((3, 16, LANES), f32),
                pltpu.VMEM((4, 3, 2, 8, LANES), bf16),
                pltpu.VMEM((16, NODES), f32),
                pltpu.VMEM((16, NODES), f32),
                pltpu.VMEM((16, NODES), f32),
                pltpu.VMEM((3, 16, LANES), f32),
                pltpu.VMEM((3, 16, LANES), f32),
                pltpu.VMEM((3, 16, NODES), f32),
                pltpu.VMEM((3, 16, LANES), f32),
                pltpu.VMEM((NODES, 16 * LANES), bf16),
                pltpu.VMEM((n, 16, 3 * LANES), f32),
                pltpu.VMEM((n, 16, 3 * LANES), bf16),
                pltpu.VMEM((n, 16, 3 * LANES), bf16),
                dma((4,)),
                dma((4,)),
                dma((3, 4)),
                dma((3, 4)),
                dma((n,)),
                dma((n,)),
            ],
            compiler_params=pltpu.CompilerParams(
                collective_id=0, has_side_effects=True, vmem_limit_bytes=63 * 1024 * 1024
            ),
        )
        out = call(
            velocity,
            eddy_viscosity,
            cell_owner.reshape(16, LANES),
            cell_element.reshape(16, LANES),
            cell_position.reshape(16, LANES),
            acoustic_state.reshape(4, 4, NODES),
            jnp.asarray(constant_table()),
        )
        moments = jnp.transpose(out[4:], (1, 0, 2)).reshape(1, 1, 4, 3, NODES)
        return moments, out[:4].reshape(4, 1, 1, 4, NODES)

    in_specs = (
        P(None, "gx", "gy", "gz"),
        P("gx", "gy", "gz"),
        P("gy", "gz", "gx", None),
        P("gy", "gz", "gx"),
        P("gy", "gz", "gx"),
        P(None, "gx", "gy", "gz", None),
    )
    out_specs = (P("gx", "gy", "gz", None, None), P(None, "gx", "gy", "gz", None))
    return jax.shard_map(on_device, mesh=mesh, in_specs=in_specs, out_specs=out_specs, check_vma=False)
```

```python
import functools

import jax
import jax.numpy as jnp
import numpy as np
from jax import lax
from jax.experimental import pallas as pl
from jax.experimental.pallas import tpu as pltpu
from jax.sharding import PartitionSpec as P

MESH = pl.DeviceIdType.MESH
SUB = 16
NODES = 512
LANES = 128
TILES = NODES // LANES
BLOCK = 8
GLL_POINTS = np.array(
    [
        -1.0,
        -0.8717401485096066,
        -0.5917001814331423,
        -0.2092992179024789,
        0.2092992179024789,
        0.5917001814331423,
        0.8717401485096066,
        1.0,
    ]
)
HALF_LIFT = 14.0
TIME_STEP = 0.01
COUPLING = 4.0
MOMENT_WEIGHT = 0.0625


def derivative_matrix():
    points = GLL_POINTS
    barycentric = np.ones(8)
    for j in range(8):
        for m in range(8):
            if m != j:
                barycentric[j] = barycentric[j] / (points[j] - points[m])
    matrix = np.zeros((8, 8))
    for i in range(8):
        for j in range(8):
            if i != j:
                matrix[i, j] = barycentric[j] / barycentric[i] / (points[i] - points[j])
        matrix[i, i] = -np.sum(matrix[i])
    return matrix


def basis_values():
    points = GLL_POINTS
    centres = -1.0 + (2.0 * np.arange(SUB) + 1.0) / SUB
    values = np.ones((SUB, 8))
    for j in range(8):
        for m in range(8):
            if m != j:
                values[:, j] = values[:, j] * (centres - points[m]) / (points[j] - points[m])
    return values


def constant_table():
    along = -derivative_matrix()
    along[0, 0] -= HALF_LIFT
    along[7, 7] += HALF_LIFT
    table = np.zeros((168, 2 * LANES))
    table[:128, :128] = np.kron(np.eye(2), np.kron(along, np.eye(8))).T
    table[:128, 128:] = np.kron(np.eye(16), along).T
    for j in range(TILES):
        for i in range(TILES):
            for h in range(2):
                lanes = slice(64 * h, 64 * h + 64)
                table[128 + 8 * j + 2 * i, lanes] = along[2 * j + h, 2 * i + h]
                table[129 + 8 * j + 2 * i, lanes] = along[2 * j + h, 2 * i + 1 - h]
    table[160:168, :SUB] = basis_values().T
    return table.astype(np.float32)


def each(count, body):
    if count <= 16:
        for k in range(count):
            body(k)
    else:
        lax.fori_loop(0, count, lambda k, c: (body(k), c)[1], 0)


def kernel(
    n,
    vel_hbm, visc_hbm, own_hbm, elem_hbm, pos_hbm, state_hbm, table_hbm,
    out_ref,
    vel_ref, visc_ref, own_ref, elem_ref, pos_ref, state_ref, table_ref, load_sem, z_out,
    vel_in, state0, state1, state2, left_in, right_in, y_in, z_in,
    nodes, part, psend, precv,
    vel_send_sem, vel_recv_sem, face_send_sem, face_recv_sem, part_send_sem, part_recv_sem,
):
    f32 = jnp.float32
    gx, gy, gz = lax.axis_index("gx"), lax.axis_index("gy"), lax.axis_index("gz")
    last = n - 1
    has_left, has_right = gx > 0, gx < last
    low_y, low_z = gy == 0, gz == 0
    left = {"gx": jnp.maximum(gx - 1, 0)}
    right = {"gx": jnp.minimum(gx + 1, last)}
    other_y, other_z = {"gy": 1 - gy}, {"gz": 1 - gz}

    def peer(k):
        return lax.rem(gx + 1 + k, n)

    barrier = pltpu.get_barrier_semaphore()
    each(last, lambda k: pl.semaphore_signal(barrier, inc=1, device_id={"gx": peer(k)}, device_id_type=MESH))
    pl.semaphore_signal(barrier, inc=1, device_id=other_y, device_id_type=MESH)
    pl.semaphore_signal(barrier, inc=1, device_id=other_z, device_id_type=MESH)
    loads = [
        pltpu.make_async_copy(src, dst, load_sem.at[k])
        for k, (src, dst) in enumerate(
            (
                (vel_hbm, vel_ref), (pos_hbm, pos_ref), (table_hbm, table_ref), (state_hbm, state_ref),
                (own_hbm, own_ref), (elem_hbm, elem_ref), (visc_hbm, visc_ref),
            )
        )
    ]
    for k in (1, 2, 3, 4, 5, 6, 0):
        loads[k].start()
    pl.semaphore_wait(barrier, last + 2)

    def remote(src, dst, send_sem, recv_sem, device):
        return pltpu.make_async_remote_copy(
            src_ref=src, dst_ref=dst, send_sem=send_sem, recv_sem=recv_sem, device_id=device, device_id_type=MESH
        )

    def vel_copy(slot, device):
        return remote(vel_hbm, vel_in.at[slot], vel_send_sem.at[slot], vel_recv_sem.at[slot], device)

    to_right, to_left = vel_copy(0, right), vel_copy(1, left)
    vel_y, vel_z = vel_copy(2, other_y), vel_copy(3, other_z)

    @pl.when(has_right)
    def _():
        to_right.start()

    @pl.when(has_left)
    def _():
        to_left.start()

    vel_z.start()
    vel_y.start()

    def faces(stage, state):
        ssem, rsem = face_send_sem.at[stage], face_recv_sem.at[stage]
        return (
            remote(state.at[:, NODES - LANES:], left_in.at[stage], ssem.at[0], rsem.at[0], right),
            remote(state.at[:, :LANES], right_in.at[stage], ssem.at[1], rsem.at[1], left),
            remote(state, y_in.at[stage], ssem.at[2], rsem.at[2], other_y),
            remote(z_out.at[stage], z_in.at[stage], ssem.at[3], rsem.at[3], other_z),
        )

    def start_faces(copies):
        @pl.when(has_right)
        def _():
            copies[0].start()

        @pl.when(has_left)
        def _():
            copies[1].start()

        copies[3].start()
        copies[2].start()

    def wait_recv(copies):
        @pl.when(has_left)
        def _():
            copies[0].wait_recv()

        @pl.when(has_right)
        def _():
            copies[1].wait_recv()

        copies[2].wait_recv()
        copies[3].wait_recv()

    def wait_send(copies):
        @pl.when(has_right)
        def _():
            copies[0].wait_send()

        @pl.when(has_left)
        def _():
            copies[1].wait_send()

        copies[2].wait_send()
        copies[3].wait_send()

    row_id = lax.broadcasted_iota(jnp.int32, (8, LANES), 0)
    lane_id = lax.broadcasted_iota(jnp.int32, (8, LANES), 1)
    rows16 = lax.broadcasted_iota(jnp.int32, (16, LANES), 0)
    lane16 = lax.broadcasted_iota(jnp.int32, (16, LANES), 1)
    b_id, c_id, e_id = (lane16 >> 3) & 7, lane16 & 7, rows16 & 3

    def tiles_of(ref):
        return [ref[:, LANES * j:LANES * (j + 1)] for j in range(TILES)]

    def pack_z(x, stage):
        packed = x[0]
        for j in range(TILES):
            shift = jnp.where(low_z, (j - 7) % LANES, j)
            packed = jnp.where(c_id == j, pltpu.roll(x[j], shift, 1), packed)
        z_out[stage] = packed

    loads[1].wait()
    loads[2].wait()

    basis = table_ref[160:168, :LANES]

    for row in range(16):
        position = jnp.broadcast_to(pos_ref[row:row + 1, :], (8, LANES))
        along = [
            jnp.take_along_axis(basis, index, axis=1, mode="promise_in_bounds")
            for index in (position >> 8, (position >> 4) & 15, position & 15)
        ]
        pair = along[0][:, None, :] * along[1][None, :, :]
        values = pair[:, :, None, :] * along[2][None, None, :, :]
        nodes[:, LANES * row:LANES * (row + 1)] = values.reshape(NODES, LANES).astype(jnp.bfloat16)

    loads[3].wait()
    for c in range(4):
        state0[4 * c:4 * c + 4, :] = state_ref[c]
    start = tiles_of(state0)
    pack_z(start, 0)
    faces0 = faces(0, state0)
    start_faces(faces0)
    loads[0].wait()
    for load in loads[4:]:
        load.wait()
    wait_recv((to_right, to_left, vel_y, vel_z))
    sources = [[None, None] for _ in range(3)]
    own_vel = [[vel_ref[c, x].astype(f32) for x in range(2)] for c in range(3)]
    from_left = [jnp.where(has_left, vel_in[0, c, 1].astype(f32), 0.0) for c in range(3)]
    from_right = [jnp.where(has_right, vel_in[1, c, 0].astype(f32), 0.0) for c in range(3)]
    for x in range(2):
        grads, laplace = [], []
        for c in range(3):
            centre = own_vel[c][x]
            beside_y, beside_z = vel_in[2, c, x].astype(f32), vel_in[3, c, x].astype(f32)
            plus_x = own_vel[c][1] if x == 0 else from_right[c]
            minus_x = from_left[c] if x == 0 else own_vel[c][0]
            plus_y = pltpu.roll(jnp.where(row_id == 0, jnp.where(low_y, beside_y, 0.0), centre), 7, 0)
            minus_y = pltpu.roll(jnp.where(row_id == 7, jnp.where(low_y, 0.0, beside_y), centre), 1, 0)
            plus_z = pltpu.roll(jnp.where(lane_id == 0, jnp.where(low_z, beside_z, 0.0), centre), LANES - 1, 1)
            minus_z = pltpu.roll(jnp.where(lane_id == LANES - 1, jnp.where(low_z, 0.0, beside_z), centre), 1, 1)
            grads.append((0.5 * (plus_x - minus_x), 0.5 * (plus_y - minus_y), 0.5 * (plus_z - minus_z)))
            laplace.append(plus_x + minus_x + plus_y + minus_y + plus_z + minus_z - 6.0 * centre)
        curl = (
            grads[2][1] - grads[1][2],
            grads[0][2] - grads[2][0],
            grads[1][0] - grads[0][1],
        )
        for c in range(3):
            d, e = (c + 1) % 3, (c + 2) % 3
            lamb = curl[d] * own_vel[e][x] - curl[e] * own_vel[d][x]
            value = visc_ref[x] * laplace[c] - lamb
            sources[c][x] = value.astype(jnp.bfloat16).astype(f32)

    block = min(BLOCK, n)
    owner_id = lax.broadcasted_iota(jnp.int32, (block, 16, LANES), 0) * 4

    def project(first):
        pieces = []
        for x in range(2):
            for y in range(8):
                row = 8 * x + y
                segment = own_ref[row:row + 1, :] * 4 + elem_ref[row:row + 1, :] - 4 * first
                segment = jnp.broadcast_to(segment, (16, LANES)) - (rows16 & 3)
                s = [jnp.broadcast_to(sources[c][x][y:y + 1, :], (16, LANES)) for c in range(3)]
                value = jnp.where(rows16 < 4, 0.0, jnp.where(rows16 < 8, s[0], jnp.where(rows16 < 12, s[1], s[2])))
                piece = jnp.where(segment[None] == owner_id, value[None], 0.0)
                pieces.append(piece.reshape(block * 16, LANES).astype(jnp.bfloat16))
        weighted = jnp.concatenate(pieces, axis=1)
        total = lax.dot_general(
            weighted, nodes[...], (((1,), (1,)), ((), ())), preferred_element_type=f32
        ).reshape(block, 16, NODES) * MOMENT_WEIGHT
        packed = jnp.concatenate(
            [
                jnp.concatenate(
                    [total[:, 4 * m + 4:4 * m + 8, LANES * j:LANES * (j + 1)] for j in range(TILES)], axis=1
                )
                for m in range(3)
            ],
            axis=2,
        )
        part[pl.ds(first, block)] = packed
        psend[pl.ds(first, block)] = packed.astype(jnp.bfloat16)

    if n == block:
        project(0)
    else:
        lax.fori_loop(0, n // block, lambda k, c: (project(k * block), c)[1], 0)

    def part_out(k):
        to = peer(k)
        return remote(psend.at[to], precv.at[gx], part_send_sem.at[to], part_recv_sem.at[gx], {"gx": to})

    def part_into(k):
        by = peer(k)
        return remote(psend.at[by], precv.at[by], part_send_sem.at[by], part_recv_sem.at[by], {"gx": by})

    each(last, lambda k: part_out(k).start())

    b_low, b_high, c_low, c_high = b_id == 0, b_id == 7, c_id == 0, c_id == 7
    on_bc = (b_low | b_high).astype(f32) + (c_low | c_high).astype(f32)
    first_half = lane16 < 64
    on_z = jnp.where(low_z, c_id + e_id, 10 - c_id - e_id) == 10

    def local_part(x):
        top = [t[:8] for t in x]
        swapped = [pltpu.roll(t, 64, 1) for t in top]
        both = jnp.concatenate(x, axis=0)
        within = jnp.dot(
            both, table_ref[:128, :], precision=lax.Precision.HIGHEST, preferred_element_type=f32
        )
        result = []
        for j in range(TILES):
            along_a = None
            for i in range(TILES):
                at = 128 + 8 * j + 2 * i
                term = table_ref[at:at + 1, :LANES] * top[i] + table_ref[at + 1:at + 2, :LANES] * swapped[i]
                along_a = term if along_a is None else along_a + term
            faces_here = on_bc
            if j == 0:
                faces_here = on_bc + first_half.astype(f32)
            if j == TILES - 1:
                faces_here = on_bc + 1.0 - first_half.astype(f32)
            along_b = within[16 * j:16 * j + 16, :LANES]
            along_c = within[16 * j:16 * j + 16, LANES:]
            above = jnp.where(e_id == 3, 0.0, pltpu.roll(x[j], 15, 0))
            below = jnp.where(e_id == 0, 0.0, pltpu.roll(x[j], 1, 0))
            upper = jnp.where(c_high, pltpu.roll(above, 7, 1), 0.0)
            lower = jnp.where(c_low, pltpu.roll(below, LANES - 7, 1), 0.0)
            along_c = along_c - HALF_LIFT * (upper - lower)
            result.append((along_a, along_b, along_c, upper + lower - faces_here * x[j]))
        return result

    def tendency(local, stage):
        result = []
        beside_z = pltpu.roll(z_in[stage], jnp.where(low_z, 3, 13), 0)
        for j in range(TILES):
            columns = slice(LANES * j, LANES * (j + 1))
            along_a, along_b, along_c, faces_here = local[j]
            beside_y = y_in[stage, :, columns]
            shifted = pltpu.roll(beside_y, jnp.where(low_y, 56, 72), 1)
            outer_b = jnp.where(jnp.where(low_y, b_id, 7 - b_id) == 7, shifted, 0.0)
            signed_b = jnp.where(low_y, outer_b, -outer_b)
            outer_c = jnp.where(on_z, pltpu.roll(beside_z, jnp.where(low_z, 7 - j, (LANES - j) % LANES), 1), 0.0)
            outer = outer_b + outer_c + faces_here
            if j == 0:
                outer_a = jnp.where(first_half & has_left, pltpu.roll(left_in[stage], 64, 1), 0.0)
                along_a, outer = along_a + HALF_LIFT * outer_a[:8], outer + outer_a
            if j == TILES - 1:
                outer_a = jnp.where(~first_half & has_right, pltpu.roll(right_in[stage], 64, 1), 0.0)
                along_a, outer = along_a - HALF_LIFT * outer_a[:8], outer + outer_a
            along_b = along_b - HALF_LIFT * signed_b
            along_c = along_c - HALF_LIFT * jnp.where(low_z, outer_c, -outer_c)
            swapped = jnp.concatenate(
                [along_a[4:8] + along_b[8:12] + along_c[12:16], along_a[0:4], along_b[0:4], along_c[0:4]], axis=0
            )
            result.append(swapped + HALF_LIFT * outer)
        return result

    local = local_part(start)
    wait_recv(faces0)
    change = tendency(local, 0)
    early = [start[j] + TIME_STEP * change[j] for j in range(TILES)]

    each(last, lambda k: part_into(k).wait_recv())
    forcing = part[pl.ds(gx, 1)][0]
    if n <= 16:
        for k in range(last):
            forcing = forcing + precv[pl.ds(peer(k), 1)][0].astype(f32)
    else:
        forcing = lax.fori_loop(
            0, last, lambda k, total: total + precv[pl.ds(peer(k), 1)][0].astype(f32), forcing
        )
    moments = [
        [forcing[4 * j:4 * j + 4, LANES * m:LANES * (m + 1)] for m in range(3)] for j in range(TILES)
    ]
    none = jnp.zeros((4, LANES), f32)
    push = [COUPLING * jnp.concatenate([none] + moments[j], axis=0) for j in range(TILES)]

    one = [early[j] + TIME_STEP * push[j] for j in range(TILES)]
    for j in range(TILES):
        state1[:, LANES * j:LANES * (j + 1)] = one[j]
    pack_z(one, 1)
    faces1 = faces(1, state1)
    start_faces(faces1)
    for m in range(3):
        for j in range(TILES):
            out_ref[4 + m, :, LANES * j:LANES * (j + 1)] = moments[j][m]
    local = local_part(one)
    wait_recv(faces1)
    change = tendency(local, 1)
    two = [
        0.75 * start[j] + 0.25 * (one[j] + TIME_STEP * (change[j] + push[j])) for j in range(TILES)
    ]
    for j in range(TILES):
        state2[:, LANES * j:LANES * (j + 1)] = two[j]
    pack_z(two, 2)
    faces2 = faces(2, state2)
    start_faces(faces2)
    local = local_part(two)
    wait_recv(faces2)
    change = tendency(local, 2)
    for j in range(TILES):
        final = (1.0 / 3.0) * start[j] + (2.0 / 3.0) * (two[j] + TIME_STEP * (change[j] + push[j]))
        for c in range(4):
            out_ref[c, :, LANES * j:LANES * (j + 1)] = final[4 * c:4 * c + 4]

    wait_send((to_right, to_left, vel_y, vel_z))
    wait_send(faces0)
    wait_send(faces1)
    wait_send(faces2)
    each(last, lambda k: part_out(k).wait_send())


def solution(mesh):
    n = mesh.shape["gx"]
    assert mesh.shape["gy"] == 2 and mesh.shape["gz"] == 2
    f32, bf16 = jnp.float32, jnp.bfloat16
    dma = pltpu.SemaphoreType.DMA

    def on_device(velocity, eddy_viscosity, cell_owner, cell_element, cell_position, acoustic_state):
        call = pl.pallas_call(
            functools.partial(kernel, n),
            out_shape=pltpu.VMEM((7, 4, NODES), f32),
            in_specs=[pl.BlockSpec(memory_space=pltpu.HBM)] * 7,
            out_specs=pl.BlockSpec(memory_space=pltpu.VMEM),
            scratch_shapes=[
                pltpu.VMEM((3, 2, 8, LANES), bf16),
                pltpu.VMEM((2, 8, LANES), f32),
                pltpu.VMEM((16, LANES), jnp.int32),
                pltpu.VMEM((16, LANES), jnp.int32),
                pltpu.VMEM((16, LANES), jnp.int32),
                pltpu.VMEM((4, 4, NODES), f32),
                pltpu.VMEM((168, 2 * LANES), f32),
                dma((7,)),
                pltpu.VMEM((3, 16, LANES), f32),
                pltpu.VMEM((4, 3, 2, 8, LANES), bf16),
                pltpu.VMEM((16, NODES), f32),
                pltpu.VMEM((16, NODES), f32),
                pltpu.VMEM((16, NODES), f32),
                pltpu.VMEM((3, 16, LANES), f32),
                pltpu.VMEM((3, 16, LANES), f32),
                pltpu.VMEM((3, 16, NODES), f32),
                pltpu.VMEM((3, 16, LANES), f32),
                pltpu.VMEM((NODES, 16 * LANES), bf16),
                pltpu.VMEM((n, 16, 3 * LANES), f32),
                pltpu.VMEM((n, 16, 3 * LANES), bf16),
                pltpu.VMEM((n, 16, 3 * LANES), bf16),
                dma((4,)),
                dma((4,)),
                dma((3, 4)),
                dma((3, 4)),
                dma((n,)),
                dma((n,)),
            ],
            compiler_params=pltpu.CompilerParams(
                collective_id=0, has_side_effects=True, vmem_limit_bytes=63 * 1024 * 1024
            ),
        )
        out = call(
            velocity,
            eddy_viscosity,
            cell_owner.reshape(16, LANES),
            cell_element.reshape(16, LANES),
            cell_position.reshape(16, LANES),
            acoustic_state.reshape(4, 4, NODES),
            jnp.asarray(constant_table()),
        )
        moments = jnp.transpose(out[4:], (1, 0, 2)).reshape(1, 1, 4, 3, NODES)
        return moments, out[:4].reshape(4, 1, 1, 4, NODES)

    in_specs = (
        P(None, "gx", "gy", "gz"),
        P("gx", "gy", "gz"),
        P("gy", "gz", "gx", None),
        P("gy", "gz", "gx"),
        P("gy", "gz", "gx"),
        P(None, "gx", "gy", "gz", None),
    )
    out_specs = (P("gx", "gy", "gz", None, None), P(None, "gx", "gy", "gz", None))
    return jax.shard_map(on_device, mesh=mesh, in_specs=in_specs, out_specs=out_specs, check_vma=False)
```
